32 devices in a mesh: dp: 16 (over z, y, core), replica: 2 (over x).
Axes of the slice: x: 2, y: 2, z: 4, core: 2. Of those that a mesh axis runs over, the one named last changes fastest.
Arguments:
- img_emb: bfloat16 [2, 2048, 768], P('replica', 'dp')
- txt_base: bfloat16 [2, 2048, 768], P('replica', 'dp')
- txt_feat: bfloat16 [2, 2048, 640], P('replica', 'dp'), may hold values from -6 to 6
- head: float32 [640, 768], P('dp'), may hold values from -0.25 to 0.25
- momentum: float32 [640, 768], P('dp'), may hold values from -3 to 3
- positive_image: int32 [2, 2048], P('replica', 'dp'), may hold values from 0 to 2047, each once within a row
Outputs:
- new_head: float32 [640, 768], P('dp')
- new_momentum: float32 [640, 768], P('dp')
The draws below stay inside these ranges and needn't reach their ends.
Inputs may be any that keep to these rules, and one draw needn't show every extreme that they name: `positive_image`: in each replica the 2048 texts name 2048 different images.
All inputs are finite; a program needn't handle non-finite values.
Results may differ from the reference program's by a relative error of at most 0.005.
Values may be sent and summed in bfloat16 or wider, within the bound.
No kernel may reach another device: no remote copies, remote signals or barrier semaphores. Data moves between devices by JAX's collectives and lax.ppermute only.
A program may use at most 64 MiB of HBM per device.

```python
import jax
import jax.numpy as jnp
from jax import lax

D = 768
K = 640
PAIRS_DEV = 128
PAIRS = 2048
REPLICAS = 2
N_DP = 16


def draw_img_emb(key, part):
    key = jax.random.fold_in(key, 11)
    return jax.random.normal(key, (REPLICAS, PAIRS, D), jnp.float32).astype(jnp.bfloat16)


def draw_txt_base(key, part):
    key = jax.random.fold_in(key, 12)
    return jax.random.normal(key, (REPLICAS, PAIRS, D), jnp.float32).astype(jnp.bfloat16)


def shard_levels(rng, dims, shards, low, largest):
    loudness = 1.0
    for position, blocks in shards:
        draws = jax.random.uniform(jax.random.fold_in(jax.random.fold_in(rng, 6), position), (blocks,), jnp.float32, low / len(shards), largest / len(shards))
        loudness = loudness * jnp.repeat(jnp.exp(draws), dims[position] // blocks).reshape((-1,) + (1,) * (len(dims) - 1 - position))
    return loudness


def centred(stream_key, dims, deviation, bound, shards=(), kind=jnp.bfloat16):
    result = deviation * jax.random.normal(stream_key, dims, jnp.float32)
    if shards:
        result = result * shard_levels(stream_key, dims, shards, -0.22, 0.18)
    return jnp.clip(result, -bound, bound).astype(kind)


def setup_inputs(seed: int = 0) -> dict:
    splits = jax.random.split(jax.random.key(seed), 7)
    img_emb = draw_img_emb(jax.random.fold_in(splits[6], 71), 0)
    txt_base = draw_txt_base(jax.random.fold_in(splits[6], 71), 0)
    txt_feat = centred(splits[2], (REPLICAS, PAIRS, K), 1.0, 6.0, ((0, 2), (1, 16)))
    head = centred(splits[3], (K, D), K ** -0.5, 0.25, ((0, 16),), jnp.float32)
    momentum = centred(splits[4], (K, D), 0.5, 3.0, ((0, 16),), jnp.float32)
    positive_image = jax.vmap(lambda own: jax.random.permutation(own, PAIRS))(jax.random.split(splits[5], REPLICAS)).reshape((REPLICAS, PAIRS)).astype(jnp.int32)
    return dict(img_emb=img_emb, txt_base=txt_base, txt_feat=txt_feat, head=head, momentum=momentum, positive_image=positive_image)


logit_scale = 10.0
logit_bias = -3.0
norm_epsilon = 1e-06
momentum_decay = 0.9
blend_weight = 0.7
outer_rate = 0.7

def reference(img_emb, txt_base, txt_feat, head, momentum, positive_image):
    head_low = head.astype(jnp.bfloat16)

    def one_replica(inputs):
        images, base, features, labels = inputs
        image_wide = images.astype(jnp.float32)
        image_unit = (image_wide * lax.rsqrt(lax.optimization_barrier(jnp.sum(image_wide * image_wide, axis=1, keepdims=True)) + norm_epsilon)).astype(jnp.bfloat16)
        text_emb = base.astype(jnp.float32) + jnp.dot(features, head_low, preferred_element_type=jnp.float32)
        inv_norm = lax.rsqrt(lax.optimization_barrier(jnp.sum(text_emb * text_emb, axis=1, keepdims=True)) + norm_epsilon)
        text_exact = text_emb * inv_norm
        text_unit = text_exact.astype(jnp.bfloat16)
        blocks = (text_unit.reshape(N_DP, PAIRS_DEV, D), labels.reshape(N_DP, PAIRS_DEV))
        columns = jnp.arange(PAIRS, dtype=jnp.int32)

        def block_grad(item):
            rows, targets = item
            logits = logit_scale * lax.dot_general(rows, image_unit, (((1,), (1,)), ((), ())), preferred_element_type=jnp.float32) + logit_bias
            matches = (targets[:, None] == columns[None, :]).astype(jnp.float32)
            weights = (jax.nn.sigmoid(logits) - matches).astype(jnp.bfloat16)
            return jnp.dot(weights, image_unit, preferred_element_type=jnp.float32)
        unit_grad = logit_scale * lax.map(block_grad, blocks).reshape(PAIRS, D)
        along = lax.optimization_barrier(jnp.sum(text_exact * unit_grad, axis=1, keepdims=True))
        text_grad = ((unit_grad - text_exact * along) * inv_norm).astype(jnp.bfloat16)
        return lax.dot_general(features, text_grad, (((0,), (0,)), ((), ())), preferred_element_type=jnp.float32)
    grads = lax.map(one_replica, (img_emb, txt_base, txt_feat, positive_image))
    head_grad = lax.optimization_barrier(jnp.sum(grads, axis=0)) / REPLICAS
    new_momentum = momentum_decay * momentum + (1.0 - momentum_decay) * head_grad
    new_head = head - outer_rate * ((1.0 - blend_weight) * head_grad + blend_weight * new_momentum)
    return (new_head, new_momentum)
```

```python
import jax
import jax.numpy as jnp
from jax import lax
from jax.experimental import pallas as pl
from jax.experimental.pallas import tpu as pltpu
from jax.sharding import PartitionSpec as P

logit_scale = 10.0
logit_bias = -3.0
norm_epsilon = 1e-06
momentum_decay = 0.9
blend_weight = 0.7
outer_rate = 0.7
label_bits = 6
bf16, f32 = jnp.bfloat16, jnp.float32


def local_kernel(body, outs, flops, scratch=(), **more):
    return pl.pallas_call(
        body,
        out_shape=outs,
        scratch_shapes=scratch,
        **more,
        compiler_params=pltpu.CompilerParams(vmem_limit_bytes=24 * 2**20),
        cost_estimate=pl.CostEstimate(flops=flops, bytes_accessed=2**10, transcendentals=0),
    )


def pack(feat_ref, base_ref, label_ref, head_ref, text_ref, low_ref, lane_ref, wide_ref, sems):
    pairs, k_size = feat_ref.shape
    width = base_ref.shape[1]
    copies = [
        pltpu.make_async_copy(head_ref, wide_ref, sems.at[0]),
        pltpu.make_async_copy(label_ref, lane_ref, sems.at[1]),
        pltpu.make_async_copy(feat_ref, text_ref.at[:, :k_size], sems.at[2]),
        pltpu.make_async_copy(base_ref, text_ref.at[:, k_size : k_size + width], sems.at[3]),
    ]
    for copy in copies:
        copy.start()
    copies[0].wait()
    low_ref[...] = wide_ref[...].astype(bf16)
    copies[1].wait()
    labels = jnp.broadcast_to(lane_ref[...].astype(f32), (pairs, pairs)).T.astype(jnp.int32)
    lane = lax.broadcasted_iota(jnp.int32, (pairs, pairs), 1)
    coded = jnp.where(lane < pairs // 2, labels >> label_bits, labels & (2**label_bits - 1))
    text_ref[:, k_size + width :] = coded.astype(f32).astype(bf16)
    for copy in copies[2:]:
        copy.wait()


def side_by_side(*refs):
    *parts, out_ref = refs
    for k, ref in enumerate(parts):
        out_ref[k] = ref[...]


def feature_part(own_ref, y_ref, c_ref, yc_ref, row_ref, column_ref, feat_ref, turned_ref):
    k_size = row_ref.shape[1]
    numbers = lax.broadcasted_iota(jnp.int32, (k_size, k_size), 0)
    order = (numbers == row_ref[...]).astype(f32).astype(bf16)
    numbers = lax.broadcasted_iota(jnp.int32, (k_size, k_size), 1)
    turned = (numbers == column_ref[...]).astype(f32).astype(bf16)
    feat = jnp.concatenate([ref[:, :k_size] for ref in (own_ref, y_ref, c_ref, yc_ref)])
    feat_ref[...] = jnp.dot(feat, order, preferred_element_type=f32).astype(bf16)
    turned_ref[...] = lax.dot_general(
        turned, feat, (((1,), (1,)), ((), ())), preferred_element_type=f32
    ).astype(bf16)


def text_part(own_ref, y_ref, c_ref, yc_ref, feat_ref, head_ref, unit_ref, exact_ref, inv_ref):
    k_size, width = head_ref.shape
    pairs = own_ref.shape[0]
    for part, ref in enumerate((own_ref, y_ref, c_ref, yc_ref)):
        here = slice(part * pairs, (part + 1) * pairs)
        emb = ref[:, k_size : k_size + width].astype(f32)
        emb = emb + jnp.dot(feat_ref[here, :], head_ref[...], preferred_element_type=f32)
        inv = lax.rsqrt(jnp.sum(emb * emb, axis=1, keepdims=True) + norm_epsilon)
        exact = emb * inv
        exact_ref[here, :] = exact
        unit_ref[here, :] = exact.astype(bf16)
        inv_ref[here, :] = jnp.broadcast_to(inv, (pairs, 128))


def unit_images(*refs):
    for ref, out_ref in zip(refs[: len(refs) // 2], refs[len(refs) // 2 :]):
        wide = ref[...].astype(f32)
        scale = lax.rsqrt(jnp.sum(wide * wide, axis=1, keepdims=True) + norm_epsilon)
        out_ref[...] = (wide * scale).astype(bf16)


def images_part(text_refs, unit_ref, number_ref, image_refs, out_ref, base_ref=None):
    pairs = image_refs[0].shape[0]
    code_at = text_refs[0].shape[1] - 128
    codes = jnp.concatenate([ref[:, code_at:].astype(f32) for ref in text_refs])
    targets = codes[:, :1] * 2.0**label_bits + codes[:, 64:65]
    for first in range(0, len(image_refs), 2):
        image = jnp.concatenate([ref[...] for ref in image_refs[first : first + 2]])
        here = slice(first * pairs, first * pairs + image.shape[0])
        logits = logit_scale * lax.dot_general(
            unit_ref[...], image, (((1,), (1,)), ((), ())), preferred_element_type=f32
        ) + logit_bias
        weights = jax.nn.sigmoid(logits) - (targets == number_ref[:, here]).astype(f32)
        term = jnp.dot(weights.astype(bf16), image, preferred_element_type=f32)
        if first == 0:
            out_ref[...] = term if base_ref is None else base_ref[...] + term
        else:
            out_ref[...] += term


def early_part(own_ref, y_ref, c_ref, yc_ref, unit_ref, number_ref, *refs):
    *image_refs, out_ref = refs
    images_part((own_ref, y_ref, c_ref, yc_ref), unit_ref, number_ref, image_refs, out_ref)


def late_part(own_ref, y_ref, c_ref, yc_ref, unit_ref, number_ref, early_ref, exact_ref, inv_ref, turned_ref, *refs):
    *image_refs, grad_ref, away_ref, sum_ref = refs
    images_part((own_ref, y_ref, c_ref, yc_ref), unit_ref, number_ref, image_refs, sum_ref, early_ref)
    unit_grad = logit_scale * sum_ref[...]
    exact = exact_ref[...]
    along = jnp.sum(exact * unit_grad, axis=1, keepdims=True)
    text_grad = ((unit_grad - exact * along) * inv_ref[:, :1]).astype(bf16)
    grad_ref[...] = text_grad
    half = away_ref.shape[0]
    away_ref[...] = jnp.dot(turned_ref[half:, :], text_grad, preferred_element_type=f32).astype(bf16)


def kept_part(turned_ref, grad_ref, keep_ref):
    half = keep_ref.shape[0]
    keep_ref[...] = jnp.dot(turned_ref[:half, :], grad_ref[...], preferred_element_type=f32)


def per_device(img_emb, txt_base, txt_feat, head, momentum, positive_image):
    n_dp, n_rep = lax.axis_size("dp"), lax.axis_size("replica")
    depth = n_dp // 4
    pairs, width = img_emb.shape[1:]
    rows, k_size = head.shape[0], txt_feat.shape[2]
    me, rep = lax.axis_index("dp"), lax.axis_index("replica")
    z, y, core = me // 4, (me // 2) % 2, me % 2

    def moved(array, dz=0, dy=0, dc=0, shift=0):
        perm = []
        for d in range(n_dp):
            target = d ^ (dz * 4 + dy * 2 + dc)
            for r in range(n_rep):
                perm.append((d * n_rep + r, target * n_rep + (r + shift) % n_rep))
        return lax.ppermute(array, ("dp", "replica"), perm)

    def shape(*dims, kind=bf16):
        return jax.ShapeDtypeStruct(dims, kind)

    text, low = pl.pallas_call(
        pack,
        out_shape=(shape(pairs, k_size + width + 128), shape(rows, width)),
        in_specs=[pl.BlockSpec(memory_space=pltpu.HBM)] * 4,
        scratch_shapes=[
            pltpu.VMEM((1, pairs), jnp.int32), pltpu.VMEM((rows, width), f32), pltpu.SemaphoreType.DMA((4,))
        ],
    )(txt_feat[0], txt_base[0], positive_image, head)
    text_y = moved(text, dy=1)
    line = local_kernel(side_by_side, shape(depth, rows, width), 2 * 10**10)(
        low, *[moved(low, dz=k) for k in range(1, depth)]
    )
    image_later, line = lax.optimization_barrier((img_emb[0], line))

    text_c = moved(lax.optimization_barrier((text, line))[0], dc=1)
    line_y = moved(line, dy=1)
    text_yc = moved(text_y, dc=1)
    chip = jnp.stack([line, line_y], axis=1).reshape(k_size // 2, width)
    place = lax.iota(jnp.int32, k_size)
    rel_c, rel_z, rel_y = place // (k_size // 2), (place // (rows * 2)) % depth, (place // rows) % 2
    owner = ((z ^ rel_z) * 2 + (y ^ rel_y)) * 2 + (core ^ rel_c)
    true_row = owner * rows + place % rows
    n_text = 4 * pairs
    packed = (text, text_y, text_c, text_yc)
    feats, turned = local_kernel(
        feature_part, (shape(n_text, k_size), shape(k_size, n_text)), 10 * n_text * k_size * k_size
    )(*packed, true_row[None, :], true_row[:, None])
    image = img_emb[0]
    held = {0: image}
    bit = depth // 2
    while bit > 1:
        held |= {k | bit: moved(held[k], dz=bit) for k in sorted(held)}
        bit //= 2
    held[1] = moved(image_later, dz=1)
    units = local_kernel(unit_images, [shape(pairs, width)] * len(held), 10**10)(*held.values())
    units = dict(zip(held, units))
    n_early = len(units)
    units |= {k | 1: moved(units[k], dz=1) for k in list(units) if k > 1}
    slot = jnp.array([k for k in units for _ in range(pairs)], jnp.int32)
    units = list(units.values())
    number = (((z ^ slot) * 2 + y) * 2 + core) * pairs + lax.iota(jnp.int32, depth * pairs) % pairs

    chip, feats = lax.optimization_barrier((chip, feats))
    parts = 4
    whole = [chip] + [moved(part, dc=1) for part in jnp.split(chip, parts)]
    whole = jnp.concatenate(whole)

    unit, exact, inv = local_kernel(
        text_part,
        (shape(n_text, width), shape(n_text, width, kind=f32), shape(n_text, 128, kind=f32)),
        10**6,
    )(*packed, feats, whole)
    number = number[None, :].astype(f32)
    split = n_early * pairs
    early = local_kernel(early_part, shape(n_text, width, kind=f32), 10**6)(
        *packed, unit, number[:, :split], *units[:n_early]
    )
    text_grad, away = local_kernel(
        late_part,
        (shape(n_text, width), shape(k_size // 2, width)),
        10**6,
        (pltpu.VMEM((n_text, width), f32),),
    )(*packed, unit, number[:, split:], early, exact, inv, turned, *units[n_early:])
    keep = local_kernel(kept_part, shape(k_size // 2, width, kind=f32), n_text * width * k_size)(turned, text_grad)

    kept = (keep + moved(away, dc=1).astype(f32)).reshape(depth, 2 * rows, width)
    sent = kept.astype(bf16)
    total = kept[0]
    for block in [moved(sent[k], dz=k) for k in [*range(2, depth), 1]]:
        total = total + block.astype(f32)
    sent = total.astype(bf16)
    total = lax.reduce_precision(total, 8, 7)
    terms = []
    for shift in range(1, n_rep):
        crossed = moved(sent[rows:], dy=1, shift=shift)
        terms.append(moved(sent[:rows], shift=shift).astype(f32) + crossed.astype(f32))
    terms.insert(0, total[:rows] + moved(sent[rows:], dy=1).astype(f32))
    if n_rep > 2:
        terms = [
            sum(jnp.where((rep - shift) % n_rep == owner, terms[shift], 0.0) for shift in range(n_rep))
            for owner in range(n_rep)
        ]
    grand = sum(terms[1:], terms[0])
    head_grad = grand / n_rep
    new_momentum = momentum_decay * momentum + (1.0 - momentum_decay) * head_grad
    new_head = head - outer_rate * ((1.0 - blend_weight) * head_grad + blend_weight * new_momentum)
    return (new_head, new_momentum)


def solution(mesh):
    placed = (
        P("replica", "dp", None),
        P("replica", "dp", None),
        P("replica", "dp", None),
        P("dp", None),
        P("dp", None),
        P("replica", "dp"),
    )
    return jax.shard_map(
        per_device,
        mesh=mesh,
        in_specs=placed,
        out_specs=(P("dp", None), P("dp", None)),
        check_vma=False,
    )
```

```python
import functools

import jax
import jax.numpy as jnp
from jax import lax
from jax.experimental import pallas as pl
from jax.experimental.pallas import tpu as pltpu
from jax.sharding import PartitionSpec as P

logit_scale = 10.0
logit_bias = -3.0
norm_epsilon = 1e-06
momentum_decay = 0.9
blend_weight = 0.7
outer_rate = 0.7
label_bits = 6
bf16, f32 = jnp.bfloat16, jnp.float32


def local_kernel(body, outs, flops, scratch=(), **more):
    return pl.pallas_call(
        body,
        out_shape=outs,
        scratch_shapes=scratch,
        **more,
        compiler_params=pltpu.CompilerParams(vmem_limit_bytes=24 * 2**20),
        cost_estimate=pl.CostEstimate(flops=flops, bytes_accessed=2**10, transcendentals=0),
    )


def pack(feat_ref, base_ref, label_ref, text_ref, lane_ref, sems):
    pairs, k_size = feat_ref.shape
    width = base_ref.shape[1]
    copies = [
        pltpu.make_async_copy(label_ref, lane_ref, sems.at[0]),
        pltpu.make_async_copy(feat_ref, text_ref.at[:, :k_size], sems.at[1]),
        pltpu.make_async_copy(base_ref, text_ref.at[:, k_size : k_size + width], sems.at[2]),
    ]
    for copy in copies:
        copy.start()
    copies[0].wait()
    labels = jnp.broadcast_to(lane_ref[...].astype(f32), (pairs, pairs)).T.astype(jnp.int32)
    lane = lax.broadcasted_iota(jnp.int32, (pairs, pairs), 1)
    coded = jnp.where(lane < pairs // 2, labels >> label_bits, labels & (2**label_bits - 1))
    text_ref[:, k_size + width :] = coded.astype(f32).astype(bf16)
    for copy in copies[1:]:
        copy.wait()


def side_by_side(*refs):
    *parts, out_ref = refs
    for k, ref in enumerate(parts):
        out_ref[k] = ref[...]


def feature_part(own_ref, y_ref, c_ref, yc_ref, row_ref, feat_ref, turned_ref):
    k_size = row_ref.shape[1]
    numbers = lax.broadcasted_iota(jnp.int32, (k_size, k_size), 0)
    order = (numbers == row_ref[...]).astype(f32).astype(bf16)
    numbers = lax.broadcasted_iota(jnp.int32, (k_size, k_size), 1)
    column = jnp.broadcast_to(row_ref[...].astype(f32), (128, k_size)).T[:, :1].astype(jnp.int32)
    turned = (numbers == column).astype(f32).astype(bf16)
    feat = jnp.concatenate([ref[:, :k_size] for ref in (own_ref, y_ref, c_ref, yc_ref)])
    feat_ref[...] = jnp.dot(feat, order, preferred_element_type=f32).astype(bf16)
    turned_ref[...] = lax.dot_general(
        turned, feat, (((1,), (1,)), ((), ())), preferred_element_type=f32
    ).astype(bf16)


def text_part(own_ref, y_ref, c_ref, yc_ref, feat_ref, head_ref, unit_ref, exact_ref, inv_ref):
    k_size, width = head_ref.shape
    pairs = own_ref.shape[0]
    for part, ref in enumerate((own_ref, y_ref, c_ref, yc_ref)):
        here = slice(part * pairs, (part + 1) * pairs)
        emb = ref[:, k_size : k_size + width].astype(f32)
        emb = emb + jnp.dot(feat_ref[here, :], head_ref[...], preferred_element_type=f32)
        inv = lax.rsqrt(jnp.sum(emb * emb, axis=1, keepdims=True) + norm_epsilon)
        exact = emb * inv
        exact_ref[here, :] = exact
        unit_ref[here, :] = exact.astype(bf16)
        inv_ref[here, :] = jnp.broadcast_to(inv, (pairs, 128))


def unit_images(*refs):
    for ref, out_ref in zip(refs[: len(refs) // 2], refs[len(refs) // 2 :]):
        wide = ref[...].astype(f32)
        scale = lax.rsqrt(jnp.sum(wide * wide, axis=1, keepdims=True) + norm_epsilon)
        out_ref[...] = (wide * scale).astype(bf16)


def images_part(keys, text_refs, unit_ref, me_ref, image_refs, out_ref, base_ref=None):
    pairs = image_refs[0].shape[0]
    code_at = text_refs[0].shape[1] - 128
    codes = jnp.concatenate([ref[:, code_at:].astype(f32) for ref in text_refs])
    targets = codes[:, :1] * 2.0**label_bits + codes[:, 64:65]
    lane = lax.broadcasted_iota(jnp.int32, (1, pairs), 1)
    for first in range(0, len(image_refs), 2):
        image = jnp.concatenate([ref[...] for ref in image_refs[first : first + 2]])
        number = jnp.concatenate(
            [(me_ref[...] ^ (4 * k)) * pairs + lane for k in keys[first : first + 2]], axis=1
        ).astype(f32)
        logits = logit_scale * lax.dot_general(
            unit_ref[...], image, (((1,), (1,)), ((), ())), preferred_element_type=f32
        ) + logit_bias
        weights = jax.nn.sigmoid(logits) - (targets == number).astype(f32)
        term = jnp.dot(weights.astype(bf16), image, preferred_element_type=f32)
        if first == 0:
            out_ref[...] = term if base_ref is None else base_ref[...] + term
        else:
            out_ref[...] += term


def early_part(keys, own_ref, y_ref, c_ref, yc_ref, unit_ref, me_ref, *refs):
    *image_refs, out_ref = refs
    images_part(keys, (own_ref, y_ref, c_ref, yc_ref), unit_ref, me_ref, image_refs, out_ref)


def late_part(keys, own_ref, y_ref, c_ref, yc_ref, unit_ref, me_ref, early_ref, exact_ref, inv_ref, turned_ref, *refs):
    *image_refs, grad_ref, away_ref, sum_ref = refs
    images_part(keys, (own_ref, y_ref, c_ref, yc_ref), unit_ref, me_ref, image_refs, sum_ref, early_ref)
    unit_grad = logit_scale * sum_ref[...]
    exact = exact_ref[...]
    along = jnp.sum(exact * unit_grad, axis=1, keepdims=True)
    text_grad = ((unit_grad - exact * along) * inv_ref[:, :1]).astype(bf16)
    grad_ref[...] = text_grad
    half = away_ref.shape[0]
    away_ref[...] = jnp.dot(turned_ref[half:, :], text_grad, preferred_element_type=f32).astype(bf16)


def kept_part(turned_ref, grad_ref, keep_ref):
    half = keep_ref.shape[0]
    keep_ref[...] = jnp.dot(turned_ref[:half, :], grad_ref[...], preferred_element_type=f32)


def per_device(img_emb, txt_base, txt_feat, head, momentum, positive_image):
    n_dp, n_rep = lax.axis_size("dp"), lax.axis_size("replica")
    depth = n_dp // 4
    pairs, width = img_emb.shape[1:]
    rows, k_size = head.shape[0], txt_feat.shape[2]
    me, rep = lax.axis_index("dp"), lax.axis_index("replica")
    z, y, core = me // 4, (me // 2) % 2, me % 2

    def moved(array, dz=0, dy=0, dc=0, shift=0):
        perm = []
        for d in range(n_dp):
            target = d ^ (dz * 4 + dy * 2 + dc)
            for r in range(n_rep):
                perm.append((d * n_rep + r, target * n_rep + (r + shift) % n_rep))
        return lax.ppermute(array, ("dp", "replica"), perm)

    def shape(*dims, kind=bf16):
        return jax.ShapeDtypeStruct(dims, kind)

    low = head.astype(bf16)
    text = pl.pallas_call(
        pack,
        out_shape=shape(pairs, k_size + width + 128),
        in_specs=[pl.BlockSpec(memory_space=pltpu.HBM)] * 3,
        scratch_shapes=[pltpu.VMEM((1, pairs), jnp.int32), pltpu.SemaphoreType.DMA((3,))],
    )(txt_feat[0], txt_base[0], positive_image)
    text_y = moved(text, dy=1)
    place = lax.iota(jnp.int32, k_size)
    rel_c, rel_z, rel_y = place // (k_size // 2), (place // (rows * 2)) % depth, (place // rows) % 2
    owner = ((z ^ rel_z) * 2 + (y ^ rel_y)) * 2 + (core ^ rel_c)
    true_row = owner * rows + place % rows

    keys, bit = [0], depth // 2
    while bit > 1:
        keys += [k | bit for k in sorted(keys)]
        bit //= 2
    keys.append(1)
    keys += [k | 1 for k in keys if k > 1]
    true_row = true_row[None, :]
    me_row = jnp.full((1, pairs), me, jnp.int32)
    line = local_kernel(side_by_side, shape(depth, rows, width), 2 * 10**10)(
        low, *[moved(low, dz=k) for k in range(1, depth)]
    )
    image_later, line = lax.optimization_barrier((img_emb[0], line))

    text_c = moved(lax.optimization_barrier((text, line))[0], dc=1)
    line_y = moved(line, dy=1)
    text_y, me_row, true_row = lax.optimization_barrier((text_y, me_row, true_row))
    text_yc = moved(text_y, dc=1)
    chip = jnp.stack([line, line_y], axis=1).reshape(k_size // 2, width)
    n_text = 4 * pairs
    packed = (text, text_y, text_c, text_yc)
    feats, turned = local_kernel(
        feature_part, (shape(n_text, k_size), shape(k_size, n_text)), 10 * n_text * k_size * k_size
    )(*packed, true_row)
    held = {0: image_later}
    bit = depth // 2
    while bit > 1:
        held |= {k | bit: moved(held[k], dz=bit) for k in sorted(held)}
        bit //= 2
    held[1] = moved(image_later, dz=1)
    units = local_kernel(unit_images, [shape(pairs, width)] * len(held), 10**10)(*held.values())
    units = dict(zip(held, units))
    n_early = len(units)
    units |= {k | 1: moved(units[k], dz=1) for k in list(units) if k > 1}
    assert list(units) == keys
    units = list(units.values())

    chip, feats = lax.optimization_barrier((chip, feats))
    parts = 4
    whole = [chip] + [moved(part, dc=1) for part in jnp.split(chip, parts)]
    whole = jnp.concatenate(whole)

    unit, exact, inv = local_kernel(
        text_part,
        (shape(n_text, width), shape(n_text, width, kind=f32), shape(n_text, 128, kind=f32)),
        10**6,
    )(*packed, feats, whole)
    early = local_kernel(functools.partial(early_part, keys[:n_early]), shape(n_text, width, kind=f32), 10**6)(
        *packed, unit, me_row, *units[:n_early]
    )
    text_grad, away = local_kernel(
        functools.partial(late_part, keys[n_early:]),
        (shape(n_text, width), shape(k_size // 2, width)),
        10**6,
        (pltpu.VMEM((n_text, width), f32),),
    )(*packed, unit, me_row, early, exact, inv, turned, *units[n_early:])
    keep = local_kernel(kept_part, shape(k_size // 2, width, kind=f32), n_text * width * k_size)(turned, text_grad)

    kept = (keep + moved(away, dc=1).astype(f32)).reshape(depth, 2 * rows, width)
    sent = kept.astype(bf16)
    total = kept[0]
    for block in [moved(sent[k], dz=k) for k in [*range(2, depth), 1]]:
        total = total + block.astype(f32)
    sent = total.astype(bf16)
    total = lax.reduce_precision(total, 8, 7)
    terms = []
    for shift in range(1, n_rep):
        crossed = moved(sent[rows:], dy=1, shift=shift)
        terms.append(moved(sent[:rows], shift=shift).astype(f32) + crossed.astype(f32))
    terms.insert(0, total[:rows] + moved(sent[rows:], dy=1).astype(f32))
    if n_rep > 2:
        terms = [
            sum(jnp.where((rep - shift) % n_rep == owner, terms[shift], 0.0) for shift in range(n_rep))
            for owner in range(n_rep)
        ]
    grand = sum(terms[1:], terms[0])
    head_grad = grand / n_rep
    new_momentum = momentum_decay * momentum + (1.0 - momentum_decay) * head_grad
    new_head = head - outer_rate * ((1.0 - blend_weight) * head_grad + blend_weight * new_momentum)
    return (new_head, new_momentum)


def solution(mesh):
    placed = (
        P("replica", "dp", None),
        P("replica", "dp", None),
        P("replica", "dp", None),
        P("dp", None),
        P("dp", None),
        P("replica", "dp"),
    )
    return jax.shard_map(
        per_device,
        mesh=mesh,
        in_specs=placed,
        out_specs=(P("dp", None), P("dp", None)),
        check_vma=False,
    )
```

```python
import functools

import jax
import jax.numpy as jnp
from jax import lax
from jax.experimental import pallas as pl
from jax.experimental.pallas import tpu as pltpu
from jax.sharding import PartitionSpec as P

logit_scale = 10.0
logit_bias = -3.0
norm_epsilon = 1e-06
momentum_decay = 0.9
blend_weight = 0.7
outer_rate = 0.7
label_bits = 6
bf16, f32 = jnp.bfloat16, jnp.float32


def local_kernel(body, outs, flops, scratch=(), **more):
    return pl.pallas_call(
        body,
        out_shape=outs,
        scratch_shapes=scratch,
        **more,
        compiler_params=pltpu.CompilerParams(vmem_limit_bytes=24 * 2**20),
        cost_estimate=pl.CostEstimate(flops=flops, bytes_accessed=2**10, transcendentals=0),
    )


def pack(feat_ref, base_ref, label_ref, text_ref, lane_ref, sems):
    pairs, k_size = feat_ref.shape
    width = base_ref.shape[1]
    copies = [
        pltpu.make_async_copy(label_ref, lane_ref, sems.at[0]),
        pltpu.make_async_copy(feat_ref, text_ref.at[:, :k_size], sems.at[1]),
        pltpu.make_async_copy(base_ref, text_ref.at[:, k_size : k_size + width], sems.at[2]),
    ]
    for copy in copies:
        copy.start()
    copies[0].wait()
    labels = jnp.broadcast_to(lane_ref[...].astype(f32), (pairs, pairs)).T.astype(jnp.int32)
    lane = lax.broadcasted_iota(jnp.int32, (pairs, pairs), 1)
    coded = jnp.where(lane < pairs // 2, labels >> label_bits, labels & (2**label_bits - 1))
    text_ref[:, k_size + width :] = coded.astype(f32).astype(bf16)
    for copy in copies[1:]:
        copy.wait()


def side_by_side(*refs):
    *parts, out_ref = refs
    for k, ref in enumerate(parts):
        out_ref[k] = ref[...]


def row_orders(row_ref, order_ref, other_ref):
    k_size = row_ref.shape[1]
    numbers = lax.broadcasted_iota(jnp.int32, (k_size, k_size), 0)
    order_ref[...] = (numbers == row_ref[...]).astype(f32).astype(bf16)
    numbers = lax.broadcasted_iota(jnp.int32, (k_size, k_size), 1)
    column = jnp.broadcast_to(row_ref[...].astype(f32), (128, k_size)).T[:, :1].astype(jnp.int32)
    other_ref[...] = (numbers == column).astype(f32).astype(bf16)


def feature_part(own_ref, y_ref, c_ref, yc_ref, order_ref, feat_ref):
    k_size = order_ref.shape[0]
    feat = jnp.concatenate([ref[:, :k_size] for ref in (own_ref, y_ref, c_ref, yc_ref)])
    feat_ref[...] = jnp.dot(feat, order_ref[...], preferred_element_type=f32).astype(bf16)


def turned_part(own_ref, y_ref, c_ref, yc_ref, other_ref, turned_ref):
    k_size = other_ref.shape[0]
    feat = jnp.concatenate([ref[:, :k_size] for ref in (own_ref, y_ref, c_ref, yc_ref)])
    turned_ref[...] = lax.dot_general(
        other_ref[...], feat, (((1,), (1,)), ((), ())), preferred_element_type=f32
    ).astype(bf16)


def text_part(own_ref, y_ref, c_ref, yc_ref, feat_ref, head_ref, unit_ref, exact_ref, inv_ref):
    k_size, width = head_ref.shape
    pairs = own_ref.shape[0]
    for part, ref in enumerate((own_ref, y_ref, c_ref, yc_ref)):
        here = slice(part * pairs, (part + 1) * pairs)
        emb = ref[:, k_size : k_size + width].astype(f32)
        emb = emb + jnp.dot(feat_ref[here, :], head_ref[...], preferred_element_type=f32)
        inv = lax.rsqrt(jnp.sum(emb * emb, axis=1, keepdims=True) + norm_epsilon)
        exact = emb * inv
        exact_ref[here, :] = exact
        unit_ref[here, :] = exact.astype(bf16)
        inv_ref[here, :] = jnp.broadcast_to(inv, (pairs, 128))


def unit_images(*refs):
    for ref, out_ref in zip(refs[: len(refs) // 2], refs[len(refs) // 2 :]):
        wide = ref[...].astype(f32)
        scale = lax.rsqrt(jnp.sum(wide * wide, axis=1, keepdims=True) + norm_epsilon)
        out_ref[...] = (wide * scale).astype(bf16)


def images_part(keys, text_refs, unit_ref, me_ref, image_refs, out_ref, base_ref=None):
    pairs = image_refs[0].shape[0]
    code_at = text_refs[0].shape[1] - 128
    codes = jnp.concatenate([ref[:, code_at:].astype(f32) for ref in text_refs])
    targets = codes[:, :1] * 2.0**label_bits + codes[:, 64:65]
    lane = lax.broadcasted_iota(jnp.int32, (1, pairs), 1)
    for first in range(0, len(image_refs), 2):
        image = jnp.concatenate([ref[...] for ref in image_refs[first : first + 2]])
        number = jnp.concatenate(
            [(me_ref[...] ^ (4 * k)) * pairs + lane for k in keys[first : first + 2]], axis=1
        ).astype(f32)
        logits = logit_scale * lax.dot_general(
            unit_ref[...], image, (((1,), (1,)), ((), ())), preferred_element_type=f32
        ) + logit_bias
        weights = jax.nn.sigmoid(logits) - (targets == number).astype(f32)
        term = jnp.dot(weights.astype(bf16), image, preferred_element_type=f32)
        if first == 0:
            out_ref[...] = term if base_ref is None else base_ref[...] + term
        else:
            out_ref[...] += term


def early_part(keys, own_ref, y_ref, c_ref, yc_ref, unit_ref, me_ref, *refs):
    *image_refs, out_ref = refs
    images_part(keys, (own_ref, y_ref, c_ref, yc_ref), unit_ref, me_ref, image_refs, out_ref)


def late_part(keys, own_ref, y_ref, c_ref, yc_ref, unit_ref, me_ref, early_ref, exact_ref, inv_ref, turned_ref, *refs):
    *image_refs, grad_ref, away_ref, sum_ref = refs
    images_part(keys, (own_ref, y_ref, c_ref, yc_ref), unit_ref, me_ref, image_refs, sum_ref, early_ref)
    unit_grad = logit_scale * sum_ref[...]
    exact = exact_ref[...]
    along = jnp.sum(exact * unit_grad, axis=1, keepdims=True)
    text_grad = ((unit_grad - exact * along) * inv_ref[:, :1]).astype(bf16)
    grad_ref[...] = text_grad
    half = away_ref.shape[0]
    away_ref[...] = jnp.dot(turned_ref[half:, :], text_grad, preferred_element_type=f32).astype(bf16)


def kept_part(turned_ref, grad_ref, keep_ref):
    half = keep_ref.shape[0]
    keep_ref[...] = jnp.dot(turned_ref[:half, :], grad_ref[...], preferred_element_type=f32)


def per_device(img_emb, txt_base, txt_feat, head, momentum, positive_image):
    n_dp, n_rep = lax.axis_size("dp"), lax.axis_size("replica")
    depth = n_dp // 4
    pairs, width = img_emb.shape[1:]
    rows, k_size = head.shape[0], txt_feat.shape[2]
    me, rep = lax.axis_index("dp"), lax.axis_index("replica")
    z, y, core = me // 4, (me // 2) % 2, me % 2

    def moved(array, dz=0, dy=0, dc=0, shift=0):
        perm = []
        for d in range(n_dp):
            target = d ^ (dz * 4 + dy * 2 + dc)
            for r in range(n_rep):
                perm.append((d * n_rep + r, target * n_rep + (r + shift) % n_rep))
        return lax.ppermute(array, ("dp", "replica"), perm)

    def shape(*dims, kind=bf16):
        return jax.ShapeDtypeStruct(dims, kind)

    low = head.astype(bf16)
    text = pl.pallas_call(
        pack,
        out_shape=shape(pairs, k_size + width + 128),
        in_specs=[pl.BlockSpec(memory_space=pltpu.HBM)] * 3,
        scratch_shapes=[pltpu.VMEM((1, pairs), jnp.int32), pltpu.SemaphoreType.DMA((3,))],
    )(txt_feat[0], txt_base[0], positive_image)
    text_y = moved(text, dy=1)
    place = lax.iota(jnp.int32, k_size)
    rel_c, rel_z, rel_y = place // (k_size // 2), (place // (rows * 2)) % depth, (place // rows) % 2
    owner = ((z ^ rel_z) * 2 + (y ^ rel_y)) * 2 + (core ^ rel_c)
    true_row = owner * rows + place % rows

    keys, bit = [0], depth // 2
    while bit > 1:
        keys += [k | bit for k in sorted(keys)]
        bit //= 2
    keys.append(1)
    keys += [k | 1 for k in keys if k > 1]
    true_row = true_row[None, :]
    me_row = jnp.full((1, pairs), me, jnp.int32)
    line = local_kernel(side_by_side, shape(depth, rows, width), 2 * 10**10)(
        low, *[moved(low, dz=k) for k in range(1, depth)]
    )
    image_later, line = lax.optimization_barrier((img_emb[0], line))

    text_c = moved(lax.optimization_barrier((text, line))[0], dc=1)
    line_y = moved(line, dy=1)
    text_y, me_row, true_row = lax.optimization_barrier((text_y, me_row, true_row))
    order, other = local_kernel(row_orders, (shape(k_size, k_size), shape(k_size, k_size)), 10**6)(true_row)
    text_y, order = lax.optimization_barrier((text_y, order))
    text_yc = moved(text_y, dc=1)
    chip = jnp.stack([line, line_y], axis=1).reshape(k_size // 2, width)
    n_text = 4 * pairs
    packed = (text, text_y, text_c, text_yc)
    turned = local_kernel(turned_part, shape(k_size, n_text), 10**6)(*packed, other)
    feats = local_kernel(feature_part, shape(n_text, k_size), 10 * n_text * k_size * k_size)(*packed, order)
    held = {0: image_later}
    bit = depth // 2
    while bit > 1:
        held |= {k | bit: moved(held[k], dz=bit) for k in sorted(held)}
        bit //= 2
    held[1] = moved(image_later, dz=1)
    units = local_kernel(unit_images, [shape(pairs, width)] * len(held), 10**10)(*held.values())
    units = dict(zip(held, units))
    n_early = len(units)
    units |= {k | 1: moved(units[k], dz=1) for k in list(units) if k > 1}
    assert list(units) == keys
    units = list(units.values())

    chip, feats = lax.optimization_barrier((chip, feats))
    *parts, part = jnp.split(chip, 4)
    part, turned = lax.optimization_barrier((part, turned))
    whole = [chip] + [moved(part, dc=1) for part in [*parts, part]]
    whole = jnp.concatenate(whole)

    unit, exact, inv = local_kernel(
        text_part,
        (shape(n_text, width), shape(n_text, width, kind=f32), shape(n_text, 128, kind=f32)),
        10**6,
    )(*packed, feats, whole)
    early = local_kernel(functools.partial(early_part, keys[:n_early]), shape(n_text, width, kind=f32), 10**6)(
        *packed, unit, me_row, *units[:n_early]
    )
    text_grad, away = local_kernel(
        functools.partial(late_part, keys[n_early:]),
        (shape(n_text, width), shape(k_size // 2, width)),
        10**6,
        (pltpu.VMEM((n_text, width), f32),),
    )(*packed, unit, me_row, early, exact, inv, turned, *units[n_early:])
    keep = local_kernel(kept_part, shape(k_size // 2, width, kind=f32), n_text * width * k_size)(turned, text_grad)

    kept = (keep + moved(away, dc=1).astype(f32)).reshape(depth, 2 * rows, width)
    sent = kept.astype(bf16)
    total = kept[0]
    for block in [moved(sent[k], dz=k) for k in [*range(2, depth), 1]]:
        total = total + block.astype(f32)
    sent = total.astype(bf16)
    total = lax.reduce_precision(total, 8, 7)
    terms = []
    for shift in range(1, n_rep):
        crossed = moved(sent[rows:], dy=1, shift=shift)
        terms.append(moved(sent[:rows], shift=shift).astype(f32) + crossed.astype(f32))
    terms.insert(0, total[:rows] + moved(sent[rows:], dy=1).astype(f32))
    if n_rep > 2:
        terms = [
            sum(jnp.where((rep - shift) % n_rep == owner, terms[shift], 0.0) for shift in range(n_rep))
            for owner in range(n_rep)
        ]
    grand = sum(terms[1:], terms[0])
    head_grad = grand / n_rep
    new_momentum = momentum_decay * momentum + (1.0 - momentum_decay) * head_grad
    new_head = head - outer_rate * ((1.0 - blend_weight) * head_grad + blend_weight * new_momentum)
    return (new_head, new_momentum)


def solution(mesh):
    placed = (
        P("replica", "dp", None),
        P("replica", "dp", None),
        P("replica", "dp", None),
        P("dp", None),
        P("dp", None),
        P("replica", "dp"),
    )
    return jax.shard_map(
        per_device,
        mesh=mesh,
        in_specs=placed,
        out_specs=(P("dp", None), P("dp", None)),
        check_vma=False,
    )
```

```python
import functools

import jax
import jax.numpy as jnp
from jax import lax
from jax.experimental import pallas as pl
from jax.experimental.pallas import tpu as pltpu
from jax.sharding import PartitionSpec as P

logit_scale = 10.0
logit_bias = -3.0
norm_epsilon = 1e-06
momentum_decay = 0.9
blend_weight = 0.7
outer_rate = 0.7
label_bits = 6
bf16, f32 = jnp.bfloat16, jnp.float32


def local_kernel(body, outs, flops, scratch=(), **more):
    return pl.pallas_call(
        body,
        out_shape=outs,
        scratch_shapes=scratch,
        **more,
        compiler_params=pltpu.CompilerParams(vmem_limit_bytes=24 * 2**20),
        cost_estimate=pl.CostEstimate(flops=flops, bytes_accessed=2**10, transcendentals=0),
    )


def pack(feat_ref, base_ref, label_ref, text_ref, lane_ref, sems):
    pairs, k_size = feat_ref.shape
    width = base_ref.shape[1]
    copies = [
        pltpu.make_async_copy(label_ref, lane_ref, sems.at[0]),
        pltpu.make_async_copy(feat_ref, text_ref.at[:, :k_size], sems.at[1]),
        pltpu.make_async_copy(base_ref, text_ref.at[:, k_size : k_size + width], sems.at[2]),
    ]
    for copy in copies:
        copy.start()
    copies[0].wait()
    labels = jnp.broadcast_to(lane_ref[...].astype(f32), (pairs, pairs)).T.astype(jnp.int32)
    lane = lax.broadcasted_iota(jnp.int32, (pairs, pairs), 1)
    coded = jnp.where(lane < pairs // 2, labels >> label_bits, labels & (2**label_bits - 1))
    text_ref[:, k_size + width :] = coded.astype(f32).astype(bf16)
    for copy in copies[1:]:
        copy.wait()


def side_by_side(*refs):
    *parts, out_ref = refs
    for k, ref in enumerate(parts):
        out_ref[k] = ref[...]


def row_orders(row_ref, order_ref, other_ref):
    k_size = row_ref.shape[1]
    numbers = lax.broadcasted_iota(jnp.int32, (k_size, k_size), 0)
    order_ref[...] = (numbers == row_ref[...]).astype(f32).astype(bf16)
    numbers = lax.broadcasted_iota(jnp.int32, (k_size, k_size), 1)
    column = jnp.broadcast_to(row_ref[...].astype(f32), (128, k_size)).T[:, :1].astype(jnp.int32)
    other_ref[...] = (numbers == column).astype(f32).astype(bf16)


def feature_part(own_ref, y_ref, c_ref, yc_ref, order_ref, other_ref, feat_ref, turned_ref):
    k_size = order_ref.shape[0]
    feat = jnp.concatenate([ref[:, :k_size] for ref in (own_ref, y_ref, c_ref, yc_ref)])
    feat_ref[...] = jnp.dot(feat, order_ref[...], preferred_element_type=f32).astype(bf16)
    turned_ref[...] = lax.dot_general(
        other_ref[...], feat, (((1,), (1,)), ((), ())), preferred_element_type=f32
    ).astype(bf16)


def text_part(own_ref, y_ref, c_ref, yc_ref, feat_ref, head_ref, unit_ref, exact_ref, inv_ref):
    k_size, width = head_ref.shape
    pairs = own_ref.shape[0]
    for part, ref in enumerate((own_ref, y_ref, c_ref, yc_ref)):
        here = slice(part * pairs, (part + 1) * pairs)
        emb = ref[:, k_size : k_size + width].astype(f32)
        emb = emb + jnp.dot(feat_ref[here, :], head_ref[...], preferred_element_type=f32)
        inv = lax.rsqrt(jnp.sum(emb * emb, axis=1, keepdims=True) + norm_epsilon)
        exact = emb * inv
        exact_ref[here, :] = exact
        unit_ref[here, :] = exact.astype(bf16)
        inv_ref[here, :] = jnp.broadcast_to(inv, (pairs, 128))


def unit_images(*refs):
    for ref, out_ref in zip(refs[: len(refs) // 2], refs[len(refs) // 2 :]):
        wide = ref[...].astype(f32)
        scale = lax.rsqrt(jnp.sum(wide * wide, axis=1, keepdims=True) + norm_epsilon)
        out_ref[...] = (wide * scale).astype(bf16)


def images_part(keys, text_refs, unit_ref, me_ref, image_refs, out_ref, base_ref=None):
    pairs = image_refs[0].shape[0]
    code_at = text_refs[0].shape[1] - 128
    codes = jnp.concatenate([ref[:, code_at:].astype(f32) for ref in text_refs])
    targets = codes[:, :1] * 2.0**label_bits + codes[:, 64:65]
    lane = lax.broadcasted_iota(jnp.int32, (1, pairs), 1)
    for first in range(0, len(image_refs), 2):
        image = jnp.concatenate([ref[...] for ref in image_refs[first : first + 2]])
        number = jnp.concatenate(
            [(me_ref[...] ^ (4 * k)) * pairs + lane for k in keys[first : first + 2]], axis=1
        ).astype(f32)
        logits = logit_scale * lax.dot_general(
            unit_ref[...], image, (((1,), (1,)), ((), ())), preferred_element_type=f32
        ) + logit_bias
        weights = jax.nn.sigmoid(logits) - (targets == number).astype(f32)
        term = jnp.dot(weights.astype(bf16), image, preferred_element_type=f32)
        if first == 0:
            out_ref[...] = term if base_ref is None else base_ref[...] + term
        else:
            out_ref[...] += term


def early_part(keys, own_ref, y_ref, c_ref, yc_ref, unit_ref, me_ref, *refs):
    *image_refs, out_ref = refs
    images_part(keys, (own_ref, y_ref, c_ref, yc_ref), unit_ref, me_ref, image_refs, out_ref)


def late_part(keys, own_ref, y_ref, c_ref, yc_ref, unit_ref, me_ref, early_ref, exact_ref, inv_ref, turned_ref, *refs):
    *image_refs, grad_ref, away_ref, sum_ref = refs
    images_part(keys, (own_ref, y_ref, c_ref, yc_ref), unit_ref, me_ref, image_refs, sum_ref, early_ref)
    unit_grad = logit_scale * sum_ref[...]
    exact = exact_ref[...]
    along = jnp.sum(exact * unit_grad, axis=1, keepdims=True)
    text_grad = ((unit_grad - exact * along) * inv_ref[:, :1]).astype(bf16)
    grad_ref[...] = text_grad
    half = away_ref.shape[0]
    away_ref[...] = jnp.dot(turned_ref[half:, :], text_grad, preferred_element_type=f32).astype(bf16)


def kept_part(turned_ref, grad_ref, keep_ref):
    half = keep_ref.shape[0]
    keep_ref[...] = jnp.dot(turned_ref[:half, :], grad_ref[...], preferred_element_type=f32)


def per_device(img_emb, txt_base, txt_feat, head, momentum, positive_image):
    n_dp, n_rep = lax.axis_size("dp"), lax.axis_size("replica")
    depth = n_dp // 4
    pairs, width = img_emb.shape[1:]
    rows, k_size = head.shape[0], txt_feat.shape[2]
    me, rep = lax.axis_index("dp"), lax.axis_index("replica")
    z, y, core = me // 4, (me // 2) % 2, me % 2

    def moved(array, dz=0, dy=0, dc=0, shift=0):
        perm = []
        for d in range(n_dp):
            target = d ^ (dz * 4 + dy * 2 + dc)
            for r in range(n_rep):
                perm.append((d * n_rep + r, target * n_rep + (r + shift) % n_rep))
        return lax.ppermute(array, ("dp", "replica"), perm)

    def shape(*dims, kind=bf16):
        return jax.ShapeDtypeStruct(dims, kind)

    low = head.astype(bf16)
    text = pl.pallas_call(
        pack,
        out_shape=shape(pairs, k_size + width + 128),
        in_specs=[pl.BlockSpec(memory_space=pltpu.HBM)] * 3,
        scratch_shapes=[pltpu.VMEM((1, pairs), jnp.int32), pltpu.SemaphoreType.DMA((3,))],
    )(txt_feat[0], txt_base[0], positive_image)
    text_y = moved(text, dy=1)
    place = lax.iota(jnp.int32, k_size)
    rel_c, rel_z, rel_y = place // (k_size // 2), (place // (rows * 2)) % depth, (place // rows) % 2
    owner = ((z ^ rel_z) * 2 + (y ^ rel_y)) * 2 + (core ^ rel_c)
    true_row = owner * rows + place % rows

    keys, bit = [0], depth // 2
    while bit > 1:
        keys += [k | bit for k in sorted(keys)]
        bit //= 2
    keys.append(1)
    keys += [k | 1 for k in keys if k > 1]
    true_row = true_row[None, :]
    me_row = jnp.full((1, pairs), me, jnp.int32)
    line = local_kernel(side_by_side, shape(depth, rows, width), 2 * 10**10)(
        low, *[moved(low, dz=k) for k in range(1, depth)]
    )
    image_later, line = lax.optimization_barrier((img_emb[0], line))

    text_c = moved(lax.optimization_barrier((text, line))[0], dc=1)
    line_y = moved(line, dy=1)
    text_y, me_row, true_row = lax.optimization_barrier((text_y, me_row, true_row))
    order, other = local_kernel(row_orders, (shape(k_size, k_size), shape(k_size, k_size)), 10**6)(true_row)
    text_y, order = lax.optimization_barrier((text_y, order))
    text_yc = moved(text_y, dc=1)
    chip = jnp.stack([line, line_y], axis=1).reshape(k_size // 2, width)
    n_text = 4 * pairs
    packed = (text, text_y, text_c, text_yc)
    feats, turned = local_kernel(
        feature_part, (shape(n_text, k_size), shape(k_size, n_text)), 10 * n_text * k_size * k_size
    )(*packed, order, other)
    held = {0: image_later}
    bit = depth // 2
    while bit > 1:
        held |= {k | bit: moved(held[k], dz=bit) for k in sorted(held)}
        bit //= 2
    held[1] = moved(image_later, dz=1)
    units = local_kernel(unit_images, [shape(pairs, width)] * len(held), 10**10)(*held.values())
    units = dict(zip(held, units))
    n_early = len(units)
    units |= {k | 1: moved(units[k], dz=1) for k in list(units) if k > 1}
    assert list(units) == keys
    units = list(units.values())

    chip, feats = lax.optimization_barrier((chip, feats))
    parts = 4
    whole = [chip] + [moved(part, dc=1) for part in jnp.split(chip, parts)]
    whole = jnp.concatenate(whole)

    unit, exact, inv = local_kernel(
        text_part,
        (shape(n_text, width), shape(n_text, width, kind=f32), shape(n_text, 128, kind=f32)),
        10**6,
    )(*packed, feats, whole)
    early = local_kernel(functools.partial(early_part, keys[:n_early]), shape(n_text, width, kind=f32), 10**6)(
        *packed, unit, me_row, *units[:n_early]
    )
    text_grad, away = local_kernel(
        functools.partial(late_part, keys[n_early:]),
        (shape(n_text, width), shape(k_size // 2, width)),
        10**6,
        (pltpu.VMEM((n_text, width), f32),),
    )(*packed, unit, me_row, early, exact, inv, turned, *units[n_early:])
    keep = local_kernel(kept_part, shape(k_size // 2, width, kind=f32), n_text * width * k_size)(turned, text_grad)

    kept = (keep + moved(away, dc=1).astype(f32)).reshape(depth, 2 * rows, width)
    sent = kept.astype(bf16)
    total = kept[0]
    for block in [moved(sent[k], dz=k) for k in [1, *range(depth - 1, 1, -1)]]:
        total = total + block.astype(f32)
    sent = total.astype(bf16)
    total = lax.reduce_precision(total, 8, 7)
    terms = []
    for shift in range(1, n_rep):
        crossed = moved(sent[rows:], dy=1, shift=shift)
        terms.append(moved(sent[:rows], shift=shift).astype(f32) + crossed.astype(f32))
    terms.insert(0, total[:rows] + moved(sent[rows:], dy=1).astype(f32))
    if n_rep > 2:
        terms = [
            sum(jnp.where((rep - shift) % n_rep == owner, terms[shift], 0.0) for shift in range(n_rep))
            for owner in range(n_rep)
        ]
    grand = sum(terms[1:], terms[0])
    head_grad = grand / n_rep
    new_momentum = momentum_decay * momentum + (1.0 - momentum_decay) * head_grad
    new_head = head - outer_rate * ((1.0 - blend_weight) * head_grad + blend_weight * new_momentum)
    return (new_head, new_momentum)


def solution(mesh):
    placed = (
        P("replica", "dp", None),
        P("replica", "dp", None),
        P("replica", "dp", None),
        P("dp", None),
        P("dp", None),
        P("replica", "dp"),
    )
    return jax.shard_map(
        per_device,
        mesh=mesh,
        in_specs=placed,
        out_specs=(P("dp", None), P("dp", None)),
        check_vma=False,
    )
```
